32 devices in a mesh: groups: 2 (over y), dom: 4 (over z), mp: 4 (over x, core).
Axes of the slice: x: 2, y: 2, z: 4, core: 2. Of those that a mesh axis runs over, the one named last changes fastest.
Arguments:
- grid_feat: bfloat16 [8192, 227], P(('groups', 'dom')), parts along dimension 0, may hold values from -6 to 6
- mesh_base: bfloat16 [8192, 512], P(('groups', 'dom'), 'mp'), parts along dimension 0, may hold values from -6 to 6
- w_embed: bfloat16 [227, 512], P(None, 'mp'), may hold values from -0.375 to 0.375
- w_edge: bfloat16 [512, 512], P(None, 'mp'), may hold values from -0.25 to 0.25
- w_agg: bfloat16 [512, 512], P(None, 'mp'), may hold values from -0.25 to 0.25
- w_msg: bfloat16 [2, 512, 512], P(None, None, 'mp'), may hold values from -0.25 to 0.25
- w_upd: bfloat16 [2, 512, 512], P(None, None, 'mp'), may hold values from -0.25 to 0.25
- w_dec: bfloat16 [512, 512], P(None, 'mp'), may hold values from -0.25 to 0.25
- w_gup: bfloat16 [512, 512], P(None, 'mp'), may hold values from -0.25 to 0.25
- w_out: bfloat16 [512, 227], P('mp'), may hold values from -0.25 to 0.25
- enc_src: int32 [4, 2048], P('dom'), may hold values from 0 to 1023
- enc_slot: int32 [4, 2048], P('dom'), may hold values from 0 to 1279, as said below
- enc_wt: float32 [4, 2048], P('dom'), may hold values from 0.3 to 3
- enc_row: int32 [4, 256], P('dom'), may hold values from 0 to 1023
- mesh_src: int32 [4, 8192], P('dom'), may hold values from 0 to 1087, as said below
- mesh_dst: int32 [4, 8192], P('dom'), may hold values from 0 to 1023
- mesh_wt: float32 [4, 8192], P('dom'), may hold values from 0.05 to 0.5
- halo_rows: int32 [4, 64], replicated, may hold values from 0 to 1023
- dec_src: int32 [4, 3072], P('dom'), may hold values from 0 to 1151, as said below
- dec_dst: int32 [4, 3072], P('dom'), may hold values from 0 to 1023
- dec_wt: float32 [4, 3072], P('dom'), may hold values from 0.1 to 1
- dec_rows: int32 [4, 128], replicated, may hold values from 0 to 1023
Outputs:
- forecast: float32 [8192, 227], P(('groups', 'dom', 'mp')), parts along dimension 0
The draws below stay inside these ranges and needn't reach their ends.
There are 2 independent parts, one for each index of `groups`. The reference program is written for one: setup_inputs(seed, part) draws one part's arguments, and reference() takes and returns one part's arrays. A program takes and returns all parts, laid end to end along the dimension named above; an argument that names none is the same for every part. Nothing has to cross between parts.
Inputs may be any that keep to these rules, and one draw needn't show every extreme that they name: `enc_slot`: in every patch every local mesh row and every neighbour slot is the target of some edge. `mesh_src`: in every patch every local mesh row and every boundary slot sends along some edge. `dec_src`: in every patch every local mesh row and every decoding slot sends along some edge.
All inputs are finite; a program needn't handle non-finite values.
Results may differ from the reference program's by a relative error of at most 0.015.
Values may be sent and summed in bfloat16 or wider, within the bound.
A program may use at most 64 MiB of HBM per device.

```python
import math
import jax
import jax.numpy as jnp
from jax import lax

C = 227
L = 512
GD = 1024
MD = 1024
NBR = 4
CAP = 64
HB = 16
DB = 32
LAYERS = 2
PW = 1
G = 4096
M = 4096
EG = 2048
EM = 8192
ED = 3072
N_DOM = 4


def spread_targets(key, patches, count, remote, slots, local):
    keys = jax.random.split(key, patches)

    def one_patch(patch_key):
        order = jax.random.permutation(patch_key, count).astype(jnp.int32)
        beyond = local + order % slots
        nearby = (order - remote) % local
        return jnp.where(order < remote, beyond, nearby).astype(jnp.int32)
    return jax.vmap(one_patch)(keys)


def draw_enc_slot(key, part):
    key = jax.random.fold_in(key, 11)
    return spread_targets(key, N_DOM, EG, EG // 6, NBR * CAP, MD)


def draw_mesh_src(key, part):
    key = jax.random.fold_in(key, 23)
    return spread_targets(key, N_DOM, EM, EM // 6, NBR * HB, MD)


def draw_dec_src(key, part):
    key = jax.random.fold_in(key, 37)
    return spread_targets(key, N_DOM, ED, ED // 6, NBR * DB, MD)


def touch_ends(values, key, smallest, top_value):
    longest = values.shape.index(max(values.shape))
    spots = []
    for shift in (0, 1):
        where = [jax.random.randint(jax.random.fold_in(key, axis), (), 0, length) for axis, length in enumerate(values.shape)]
        where[longest] = (where[longest] + shift) % values.shape[longest]
        spots.append(tuple(where))
    return values.at[spots[0]].set(smallest).at[spots[1]].set(top_value)


def shard_levels(stream_key, dims, cuts, smallest, high):
    def one(position, parts):
        heights = jax.random.uniform(jax.random.fold_in(jax.random.fold_in(stream_key, 6), position), (parts,), jnp.float32, smallest / len(cuts), high / len(cuts))
        return jnp.repeat(jnp.exp(heights), dims[position] // parts).reshape((-1,) + (1,) * (len(dims) - position - 1))

    factor_of = one(*cuts[0])
    for cut in cuts[1:]:
        factor_of = factor_of * one(*cut)
    return factor_of


def bell_draw(key, extent, scale, most, pieces=(), kind=jnp.bfloat16):
    drawn = scale * jax.random.normal(key, extent, jnp.float32)
    if pieces:
        drawn = drawn * shard_levels(key, extent, pieces, -0.22, 0.18)
    return jnp.clip(drawn, -most, most).astype(kind)


def setup_inputs(seed: int = 0, part: int = 0) -> dict:
    seeds = jax.random.split(jax.random.key(seed), 23)
    part_keys = jax.random.split(jax.random.fold_in(seeds[22], part), 23)
    return {
        "grid_feat": bell_draw(part_keys[0], (G, C), 1.0, 6.0, ((0, 4),)),
        "mesh_base": bell_draw(part_keys[1], (M, L), 1.0, 6.0, ((0, 4), (1, 4))),
        "w_embed": bell_draw(seeds[2], (C, L), C ** -0.5, 0.375, ((1, 4),)),
        "w_edge": bell_draw(seeds[3], (L, L), L ** -0.5, 0.25, ((1, 4),)),
        "w_agg": bell_draw(seeds[4], (L, L), L ** -0.5, 0.25, ((1, 4),)),
        "w_msg": bell_draw(seeds[5], (LAYERS, L, L), L ** -0.5, 0.25, ((2, 4),)),
        "w_upd": bell_draw(seeds[6], (LAYERS, L, L), L ** -0.5, 0.25, ((2, 4),)),
        "w_dec": bell_draw(seeds[7], (L, L), L ** -0.5, 0.25, ((1, 4),)),
        "w_gup": bell_draw(seeds[8], (L, L), L ** -0.5, 0.25, ((1, 4),)),
        "w_out": bell_draw(seeds[9], (L, C), L ** -0.5, 0.25, ((0, 4),)),
        "enc_src": touch_ends(jax.random.randint(seeds[10], (N_DOM, EG), 0, GD), jax.random.fold_in(seeds[10], 1), 0, GD - 1).astype(jnp.int32),
        "enc_slot": draw_enc_slot(jax.random.fold_in(seeds[22], 71), part),
        "enc_wt": jnp.clip(jnp.exp(math.log(3.0) - 2.3025851 * jax.random.uniform(seeds[12], (N_DOM, EG), jnp.float32) ** shard_levels(seeds[12], (N_DOM, EG), ((0, 4),), -0.2, 0.2)), 0.3, 3.0),
        "enc_row": touch_ends(jax.random.randint(seeds[13], (N_DOM, NBR * CAP), 0, MD), jax.random.fold_in(seeds[13], 1), 0, MD - 1).astype(jnp.int32),
        "mesh_src": draw_mesh_src(jax.random.fold_in(seeds[22], 71), part),
        "mesh_dst": touch_ends(jax.random.randint(seeds[15], (N_DOM, EM), 0, MD), jax.random.fold_in(seeds[15], 1), 0, MD - 1).astype(jnp.int32),
        "mesh_wt": jnp.clip(jnp.exp(math.log(0.5) - 2.3025851 * jax.random.uniform(seeds[16], (N_DOM, EM), jnp.float32) ** shard_levels(seeds[16], (N_DOM, EM), ((0, 4),), -0.2, 0.2)), 0.05, 0.5),
        "halo_rows": touch_ends(jax.random.randint(seeds[17], (N_DOM, NBR * HB), 0, MD), jax.random.fold_in(seeds[17], 1), 0, MD - 1).astype(jnp.int32),
        "dec_src": draw_dec_src(jax.random.fold_in(seeds[22], 71), part),
        "dec_dst": touch_ends(jax.random.randint(seeds[19], (N_DOM, ED), 0, GD), jax.random.fold_in(seeds[19], 1), 0, GD - 1).astype(jnp.int32),
        "dec_wt": jnp.clip(jnp.exp(math.log(1.0) - 2.3025851 * jax.random.uniform(seeds[20], (N_DOM, ED), jnp.float32) ** shard_levels(seeds[20], (N_DOM, ED), ((0, 4),), -0.2, 0.2)), 0.1, 1.0),
        "dec_rows": touch_ends(jax.random.randint(seeds[21], (N_DOM, NBR * DB), 0, MD), jax.random.fold_in(seeds[21], 1), 0, MD - 1).astype(jnp.int32),
    }


def reference(grid_feat, mesh_base, w_embed, w_edge, w_agg, w_msg, w_upd, w_dec, w_gup, w_out, enc_src, enc_slot, enc_wt, enc_row, mesh_src, mesh_dst, mesh_wt, halo_rows, dec_src, dec_dst, dec_wt, dec_rows):
    owners = jnp.arange(N_DOM, dtype=jnp.int32)
    offsets = jnp.array([1, -1, PW, -PW], dtype=jnp.int32)
    grid_lat = jax.nn.silu(jnp.dot(grid_feat, w_embed, preferred_element_type=jnp.float32)).astype(jnp.bfloat16)
    sent = jax.nn.silu(jnp.dot(grid_lat, w_edge, preferred_element_type=jnp.float32)).astype(jnp.bfloat16)

    def encode_step(total, owner):
        slots = enc_slot[owner]
        beyond = jnp.maximum(slots - MD, 0)
        side = beyond // CAP
        peer_of = (owner + offsets[side]) % N_DOM
        remote = peer_of * MD + enc_row[peer_of, side * CAP + beyond % CAP]
        target = jnp.where(slots < MD, owner * MD + slots, remote)
        values = sent[owner * GD + enc_src[owner]].astype(jnp.float32) * enc_wt[owner][:, None]
        return total + jax.ops.segment_sum(values, target, num_segments=M), None

    enc_sum, _ = lax.scan(encode_step, jnp.zeros((M, L), jnp.float32), owners)
    mesh_lat = (mesh_base.astype(jnp.float32) + jax.nn.silu(jnp.dot(enc_sum.astype(jnp.bfloat16), w_agg, preferred_element_type=jnp.float32))).astype(jnp.bfloat16)
    for layer_num in range(LAYERS):
        message = jax.nn.silu(jnp.dot(mesh_lat, w_msg[layer_num], preferred_element_type=jnp.float32)).astype(jnp.bfloat16)

        def mesh_step(carry, owner):
            source = mesh_src[owner]
            beyond = jnp.maximum(source - MD, 0)
            side = beyond // HB
            peer_of = (owner - offsets[side]) % N_DOM
            remote = peer_of * MD + halo_rows[peer_of, side * HB + beyond % HB]
            global_row = jnp.where(source < MD, owner * MD + source, remote)
            values = message[global_row].astype(jnp.float32) * mesh_wt[owner][:, None]
            return carry, jax.ops.segment_sum(values, mesh_dst[owner], num_segments=MD)

        _, mesh_sum = lax.scan(mesh_step, jnp.zeros((), jnp.float32), owners)
        mesh_sum = mesh_sum.reshape(M, L)
        mesh_lat = (mesh_lat.astype(jnp.float32) + jax.nn.silu(jnp.dot(mesh_sum.astype(jnp.bfloat16), w_upd[layer_num], preferred_element_type=jnp.float32))).astype(jnp.bfloat16)
    decoded = jax.nn.silu(jnp.dot(mesh_lat, w_dec, preferred_element_type=jnp.float32)).astype(jnp.bfloat16)

    def decode_step(carry, owner):
        source = dec_src[owner]
        beyond = jnp.maximum(source - MD, 0)
        side = beyond // DB
        peer_of = (owner - offsets[side]) % N_DOM
        remote = peer_of * MD + dec_rows[peer_of, side * DB + beyond % DB]
        global_row = jnp.where(source < MD, owner * MD + source, remote)
        values = decoded[global_row].astype(jnp.float32) * dec_wt[owner][:, None]
        return carry, jax.ops.segment_sum(values, dec_dst[owner], num_segments=GD)

    _, dec_sum = lax.scan(decode_step, jnp.zeros((), jnp.float32), owners)
    dec_sum = dec_sum.reshape(G, L)
    grid_new = (grid_lat.astype(jnp.float32) + jax.nn.silu(jnp.dot(dec_sum.astype(jnp.bfloat16), w_gup, preferred_element_type=jnp.float32))).astype(jnp.bfloat16)
    return jnp.dot(grid_new, w_out, preferred_element_type=jnp.float32)
```

```python
import functools

import jax
import jax.numpy as jnp
from jax import lax
from jax.experimental import pallas as pl
from jax.experimental.pallas import tpu as pltpu
from jax.sharding import PartitionSpec as P

MESH = pl.DeviceIdType.MESH
BF = jnp.bfloat16
F32 = jnp.float32
CHUNK = 512
TILE = 256


def silu(v):
    h = 0.5 * v
    return h + h * jnp.tanh(h)


def mm(a, b):
    return jnp.dot(a, b, preferred_element_type=F32)


def mm_nt(a, b):
    return lax.dot_general(a, b, (((1,), (1,)), ((), ())), preferred_element_type=F32)


def kernel(
    n_dom,
    grid_feat, mesh_base, w_embed, w_edge, w_agg, w_msg, w_upd, w_dec, w_gup, w_out,
    enc_src, enc_slot, enc_wt, enc_row, mesh_src, mesh_dst, mesh_wt, halo_rows,
    dec_src, dec_dst, dec_wt, dec_rows,
    out,
    emb_s, wq, wo, base_s, grid_lat, sent, a_enc, acc_enc, a_mesh, acc_mesh, a_dec, acc_dec,
    pick_h, pick_d, enc_out, enc_in, esum, lat, msg, halo_out, halo_in, dec_out, dec_in,
    sib_send, sib_recv, x_send, x_recv, f_send, f_recv, b_send, b_recv,
    e_send, e_recv, h_send, h_recv, d_send, d_recv, g_send, g_recv,
):
    gd = grid_feat.shape[0]
    md = mesh_base.shape[0]
    half = md // 2
    quarter = gd // 4
    lat_w = wq.shape[2]
    cin = grid_feat.shape[1]
    cap = enc_row.shape[1] // 4
    hb = halo_rows.shape[1] // 4
    db = dec_rows.shape[1] // 4
    layers = w_msg.shape[0]
    width = n_dom // 4
    offsets = (1, n_dom - 1, width, n_dom - width)
    g = lax.axis_index("groups")
    d = lax.axis_index("dom")
    i = lax.axis_index("mp")
    c = lax.rem(i, 2)
    sib = i + 1 - 2 * c
    xp = lax.rem(i + 2, 4)
    xs = lax.rem(sib + 2, 4)

    peers = [(g, d, sib), (g, d, xp), (g, d, xs)]
    for o in sorted(set(o % n_dom for o in offsets)):
        peers.append((g, lax.rem(d + o, n_dom), i))
    barrier = pltpu.get_barrier_semaphore()
    for peer in peers:
        pl.semaphore_signal(barrier, inc=1, device_id=peer, device_id_type=MESH)

    emb_s[i] = jnp.zeros(emb_s.shape[1:], BF)
    emb_s[i, 0:cin, :] = w_embed[...]
    wo[i] = jnp.zeros(wo.shape[1:], BF)
    wo[i, :, 0:cin] = w_out[...]
    sources = [w_edge, w_agg]
    for l in range(layers):
        sources += [w_msg.at[l], w_upd.at[l]]
    sources += [w_dec, w_gup]
    n_w = len(sources)
    for k in range(n_w):
        wq[k, i] = sources[k][...]
    base_s[i] = mesh_base[pl.ds(pl.multiple_of(c * half, half), half), :]

    EMB, OUT = n_w, n_w + 1

    def slot(k, q):
        if k == EMB:
            return emb_s.at[q]
        if k == OUT:
            return wo.at[q]
        return wq.at[k, q]

    def copy(src, dst, ss, rs, dev):
        return pltpu.make_async_remote_copy(
            src_ref=src, dst_ref=dst, send_sem=ss, recv_sem=rs, device_id=dev, device_id_type=MESH
        )

    def to_sib(k):
        return copy(slot(k, i), slot(k, i), sib_send.at[k], sib_recv.at[k], (g, d, sib))

    def to_x(k):
        return copy(slot(k, i), slot(k, i), x_send.at[k], x_recv.at[k], (g, d, xp))

    def fwd(k):
        return copy(slot(k, xp), slot(k, xp), f_send.at[k], f_recv.at[k], (g, d, sib))

    my_rows = pl.ds(pl.multiple_of(c * half, half), half)
    sib_rows = pl.ds(pl.multiple_of((1 - c) * half, half), half)
    base_copies = [
        copy(mesh_base.at[sib_rows, :], base_s.at[i], b_send.at[0], b_recv.at[0], (g, d, sib)),
        copy(mesh_base.at[my_rows, :], base_s.at[i], b_send.at[1], b_recv.at[1], (g, d, xp)),
        copy(mesh_base.at[sib_rows, :], base_s.at[i], b_send.at[2], b_recv.at[2], (g, d, xs)),
    ]

    pl.semaphore_wait(barrier, len(peers))

    def launch(ks):
        for k in ks:
            to_x(k).start()
            to_sib(k).start()

    def relay(ks):
        for k in ks:
            to_x(k).wait_recv()
            fwd(k).start()

    def ready(ks):
        for k in ks:
            to_sib(k).wait_recv()
            fwd(k).wait_recv()

    launch([EMB, 0])
    for b in base_copies:
        b.start()
    launch([1])

    def build(src_ref, dst_ref, wt_ref, target_of, rows, cols, acc, lo, hi):
        def body(t, _):
            e = pl.ds(pl.multiple_of(t * CHUNK, CHUNK), CHUNK)
            tgt = target_of(lax.broadcasted_iota(jnp.int32, (rows, CHUNK), 0))
            dt = jnp.where(tgt == dst_ref[:, e], 1.0, 0.0).astype(BF)
            row = lax.broadcasted_iota(jnp.int32, (cols, CHUNK), 0)
            st = jnp.where(row == src_ref[:, e], wt_ref[:, e], 0.0).astype(BF)
            acc[...] += mm_nt(dt, st)
            return 0

        lax.fori_loop(lo, hi, body, 0)

    def enc_target(m):
        return jnp.where(m < half, m + c * half, m + (md - half))

    acc_enc[...] = jnp.zeros(acc_enc.shape, F32)
    build(enc_src, enc_slot, enc_wt, enc_target, half + 4 * cap, gd, acc_enc, 0, enc_src.shape[1] // CHUNK)
    a_enc[...] = acc_enc[...].astype(BF)

    def weight(k):
        return jnp.concatenate([wq[k, q] for q in range(4)], axis=1)

    def tiles(n, body):
        def step(t, _):
            body(pl.ds(pl.multiple_of(t * TILE, TILE), TILE))
            return 0

        lax.fori_loop(0, n // TILE, step, 0)

    relay([EMB, 0])
    ready([EMB])
    launch([2, 3])

    def embed(r):
        w = jnp.concatenate([emb_s[q] for q in range(4)], axis=1)[0:cin]
        grid_lat[r, :] = silu(mm(grid_feat[r, :], w)).astype(BF)

    tiles(gd, embed)
    ready([0])

    def edge(r):
        sent[r, :] = silu(mm(grid_lat[r, :], weight(0))).astype(BF)

    tiles(gd, edge)

    slots = pl.ds(half, 4 * cap)
    enc_out[...] = mm(a_enc[slots, :], sent[...]).astype(BF)
    enc_copies, halo_copies, dec_copies = [], [], []
    for j in range(4):
        peer = (g, lax.rem(d + offsets[j], n_dom), i)
        own = pl.ds(j * cap, cap)
        enc_copies.append(copy(enc_out.at[own, :], enc_in.at[own, :], e_send.at[j], e_recv.at[j], peer))
        enc_copies[-1].start()

    def enc_local(r):
        esum[r, :] = mm(a_enc[r, :], sent[...])

    tiles(half, enc_local)
    relay([1])

    def pick(rows_ref, ref):
        n = ref.shape[0]
        row = rows_ref[pl.ds(d, 1), :].astype(F32)
        col = jnp.broadcast_to(row, (128, n)).T
        lane = lax.broadcasted_iota(jnp.int32, (n, 128), 1).astype(F32)
        for b in range(md // 128):
            ref[:, b * 128 : (b + 1) * 128] = jnp.where(col == lane + 128.0 * b, 1.0, 0.0).astype(BF)

    pick(halo_rows, pick_h)
    pick(dec_rows, pick_d)

    acc_mesh[...] = jnp.zeros(acc_mesh.shape, F32)
    acc_dec[...] = jnp.zeros(acc_dec.shape, F32)
    mesh_chunks = mesh_src.shape[1] // CHUNK
    dec_chunks = dec_src.shape[1] // CHUNK
    mesh_cols = acc_mesh.shape[1]

    def mesh_target(m):
        return m + c * half

    def dec_target(m):
        return m + i * quarter

    def build_mesh(lo, hi):
        build(mesh_src, mesh_dst, mesh_wt, mesh_target, half, mesh_cols, acc_mesh, lo, hi)

    def build_dec(lo, hi):
        build(dec_src, dec_dst, dec_wt, dec_target, quarter, acc_dec.shape[1], acc_dec, lo, hi)

    build_mesh(0, mesh_chunks // 2)
    relay([2, 3])
    launch([4, 5])
    build_mesh(mesh_chunks // 2, mesh_chunks)
    a_mesh[...] = acc_mesh[...].astype(BF)
    relay([4, 5])
    launch([6, 7, OUT])

    for cp in enc_copies:
        cp.wait_recv()
    ready([1])
    for b in base_copies:
        b.wait_recv()

    def agg(r):
        m = lax.broadcasted_iota(jnp.int32, (TILE, 4 * cap), 0) + (c * half + r.start)
        place = jnp.where(m == enc_row[...], 1.0, 0.0).astype(BF)
        total = (esum[r, :] + mm(place, enc_in[...])).astype(BF)
        base = jnp.concatenate([base_s[q, r, :] for q in range(4)], axis=1).astype(F32)
        lat[r, :] = (base + silu(mm(total, weight(1)))).astype(BF)

    tiles(half, agg)

    share_copies = []

    def share(k, t):
        def body(r):
            there = pl.ds(pl.multiple_of(c * half + r.start, TILE), TILE)
            msg[t, there, :] = silu(mm(lat[r, :], weight(k))).astype(BF)

        tiles(half, body)
        cp = copy(msg.at[t, my_rows, :], msg.at[t, my_rows, :], g_send.at[t], g_recv.at[t], (g, d, sib))
        cp.start()
        share_copies.append(cp)
        return cp

    for l in range(layers):
        kw = 2 + 2 * l
        ready([kw])
        cp = share(kw, l)
        if l == 0:
            build_dec(0, dec_chunks // 2)
        cp.wait_recv()
        halo_out[l] = mm(pick_h[...], msg[l]).astype(BF)
        arriving = []
        for j in range(4):
            peer = (g, lax.rem(d + offsets[j], n_dom), i)
            own = pl.ds(j * hb, hb)
            arriving.append(
                copy(halo_out.at[l, own, :], halo_in.at[l, own, :], h_send.at[l, j], h_recv.at[l, j], peer)
            )
            arriving[-1].start()
        halo_copies += arriving

        def local(r, l=l):
            esum[r, :] = mm(a_mesh[r, 0:md], msg[l])

        tiles(half, local)
        if l == 0:
            build_dec(dec_chunks // 2, dec_chunks)
            a_dec[...] = acc_dec[...].astype(BF)
            relay([6, 7, OUT])
        ready([kw + 1])
        for cp in arriving:
            cp.wait_recv()

        def update(r, l=l, kw=kw):
            total = (esum[r, :] + mm(a_mesh[r, md : md + 4 * hb], halo_in[l])).astype(BF)
            lat[r, :] = (lat[r, :].astype(F32) + silu(mm(total, weight(kw + 1)))).astype(BF)

        tiles(half, update)

    kd = n_w - 2
    ready([kd])
    cp = share(kd, layers)
    ready([n_w - 1, OUT])
    cp.wait_recv()
    dec_out[...] = mm(pick_d[...], msg[layers]).astype(BF)
    for j in range(4):
        peer = (g, lax.rem(d + offsets[j], n_dom), i)
        own = pl.ds(j * db, db)
        dec_copies.append(copy(dec_out.at[own, :], dec_in.at[own, :], d_send.at[j], d_recv.at[j], peer))
        dec_copies[-1].start()
    part = mm(a_dec[:, 0:md], msg[layers])
    for cp in dec_copies:
        cp.wait_recv()
    total = (part + mm(a_dec[:, md : md + 4 * db], dec_in[...])).astype(BF)
    mine = grid_lat[pl.ds(pl.multiple_of(i * quarter, quarter), quarter), :].astype(F32)
    new = (mine + silu(mm(total, weight(n_w - 1)))).astype(BF)
    head = jnp.concatenate([wo[q] for q in range(4)], axis=0)
    out[...] = mm(new, head)[:, 0:cin]

    for k in range(n_w + 2):
        to_sib(k).wait_send()
        to_x(k).wait_send()
        fwd(k).wait_send()
    for cp in base_copies + enc_copies + halo_copies + dec_copies + share_copies:
        cp.wait_send()


def per_device(n_dom, *args):
    grid_feat, mesh_base, w_msg = args[0], args[1], args[5]
    enc_row, halo_rows, dec_rows = args[13], args[17], args[21]
    gd, cin = grid_feat.shape
    md = mesh_base.shape[0]
    layers, width = w_msg.shape[0], w_msg.shape[1]
    half, quarter = md // 2, gd // 4
    n_enc, n_halo, n_dec = enc_row.shape[1], halo_rows.shape[1], dec_rows.shape[1]
    n_w = 4 + 2 * layers
    cin_pad = -(-cin // 128) * 128
    mesh_cols = md + -(-n_halo // 128) * 128
    dec_cols = md + -(-n_dec // 128) * 128
    V = pltpu.VMEM
    dma = pltpu.SemaphoreType.DMA
    scratch = [
        V((4, cin_pad, 128), BF),
        V((n_w, 4, width, 128), BF),
        V((4, 128, cin_pad), BF),
        V((4, half, 128), BF),
        V((gd, width), BF),
        V((gd, width), BF),
        V((half + n_enc, gd), BF),
        V((half + n_enc, gd), F32),
        V((half, mesh_cols), BF),
        V((half, mesh_cols), F32),
        V((quarter, dec_cols), BF),
        V((quarter, dec_cols), F32),
        V((n_halo, md), BF),
        V((n_dec, md), BF),
        V((n_enc, width), BF),
        V((n_enc, width), BF),
        V((half, width), F32),
        V((half, width), BF),
        V((layers + 1, md, width), BF),
        V((layers, n_halo, width), BF),
        V((layers, n_halo, width), BF),
        V((n_dec, width), BF),
        V((n_dec, width), BF),
        dma((n_w + 2,)), dma((n_w + 2,)), dma((n_w + 2,)), dma((n_w + 2,)), dma((n_w + 2,)), dma((n_w + 2,)),
        dma((3,)), dma((3,)),
        dma((4,)), dma((4,)), dma((layers, 4)), dma((layers, 4)), dma((4,)), dma((4,)),
        dma((layers + 1,)), dma((layers + 1,)),
    ]
    return pl.pallas_call(
        functools.partial(kernel, n_dom),
        out_shape=jax.ShapeDtypeStruct((quarter, cin), F32),
        in_specs=[pl.BlockSpec(memory_space=V)] * len(args),
        out_specs=pl.BlockSpec(memory_space=V),
        scratch_shapes=scratch,
        compiler_params=pltpu.CompilerParams(
            collective_id=0, has_side_effects=True, vmem_limit_bytes=56 * 1024 * 1024
        ),
    )(*args)


def solution(mesh):
    in_specs = (
        P(("groups", "dom"), None),
        P(("groups", "dom"), "mp"),
        P(None, "mp"),
        P(None, "mp"),
        P(None, "mp"),
        P(None, None, "mp"),
        P(None, None, "mp"),
        P(None, "mp"),
        P(None, "mp"),
        P("mp", None),
        P("dom", None),
        P("dom", None),
        P("dom", None),
        P("dom", None),
        P("dom", None),
        P("dom", None),
        P("dom", None),
        P(),
        P("dom", None),
        P("dom", None),
        P("dom", None),
        P(),
    )
    out_specs = P(("groups", "dom", "mp"), None)
    return jax.shard_map(
        functools.partial(per_device, mesh.shape["dom"]),
        mesh=mesh,
        in_specs=in_specs,
        out_specs=out_specs,
        check_vma=False,
    )
```

```python
import functools

import jax
import jax.numpy as jnp
from jax import lax
from jax.experimental import pallas as pl
from jax.experimental.pallas import tpu as pltpu
from jax.sharding import PartitionSpec as P

MESH = pl.DeviceIdType.MESH
BF = jnp.bfloat16
F32 = jnp.float32
CHUNK = 2048
TILE = 256


def silu(v):
    h = 0.5 * v
    return h + h * jnp.tanh(h)


def mm(a, b):
    return jnp.dot(a, b, preferred_element_type=F32)


def mm_tn(a, b):
    return lax.dot_general(a, b, (((0,), (0,)), ((), ())), preferred_element_type=F32)


def mm_nt(a, b):
    return lax.dot_general(a, b, (((1,), (1,)), ((), ())), preferred_element_type=F32)


def kernel(
    n_dom,
    grid_feat, mesh_base, w_embed, w_edge, w_agg, w_msg, w_upd, w_dec, w_gup, w_out,
    enc_src, enc_slot, enc_wt, enc_row, mesh_src, mesh_dst, mesh_wt, halo_rows,
    dec_src, dec_dst, dec_wt, dec_rows,
    out,
    emb_s, wq, wo, base_s, grid_lat, sent, a_enc, acc_enc, a_mesh, acc_mesh, a_dec, acc_dec,
    pick_h, pick_d, enc_out, enc_in, esum, lat, msg, halo_out, halo_in, dec_out, dec_in,
    sib_send, sib_recv, x_send, x_recv, f_send, f_recv, b_send, b_recv,
    e_send, e_recv, h_send, h_recv, d_send, d_recv, g_send, g_recv,
):
    cin, gd = grid_feat.shape
    md = mesh_base.shape[0]
    half = md // 2
    quarter = gd // 4
    lat_w = wq.shape[2]
    cap = enc_row.shape[1] // 4
    hb = halo_rows.shape[1] // 4
    db = dec_rows.shape[1] // 4
    layers = w_msg.shape[0]
    width = n_dom // 4
    offsets = (1, n_dom - 1, width, n_dom - width)
    g = lax.axis_index("groups")
    d = lax.axis_index("dom")
    i = lax.axis_index("mp")
    c = lax.rem(i, 2)
    sib = i + 1 - 2 * c
    xp = lax.rem(i + 2, 4)
    xs = lax.rem(sib + 2, 4)

    peers = [(g, d, sib), (g, d, xp), (g, d, xs)]
    for o in sorted(set(o % n_dom for o in offsets)):
        peers.append((g, lax.rem(d + o, n_dom), i))
    barrier = pltpu.get_barrier_semaphore()
    for peer in peers:
        pl.semaphore_signal(barrier, inc=1, device_id=peer, device_id_type=MESH)

    emb_s[i] = jnp.zeros(emb_s.shape[1:], BF)
    emb_s[i, 0:cin, :] = w_embed[...]
    wo[i] = jnp.zeros(wo.shape[1:], BF)
    wo[i, 0:cin, :] = w_out[...]
    sources = [w_edge, w_agg]
    for l in range(layers):
        sources += [w_msg.at[l], w_upd.at[l]]
    sources += [w_dec, w_gup]
    n_w = len(sources)

    EMB, OUT = n_w, n_w + 1

    def slot(k, q):
        if k == EMB:
            return emb_s.at[q]
        if k == OUT:
            return wo.at[q]
        return wq.at[k, q]

    def copy(src, dst, ss, rs, dev):
        return pltpu.make_async_remote_copy(
            src_ref=src, dst_ref=dst, send_sem=ss, recv_sem=rs, device_id=dev, device_id_type=MESH
        )

    def own(k):
        return sources[k] if k < n_w else slot(k, i)

    def to_sib(k):
        return copy(own(k), slot(k, i), sib_send.at[k], sib_recv.at[k], (g, d, sib))

    def to_x(k):
        return copy(own(k), slot(k, i), x_send.at[k], x_recv.at[k], (g, d, xp))

    def fwd(k):
        return copy(slot(k, xp), slot(k, xp), f_send.at[k], f_recv.at[k], (g, d, sib))

    my_rows = pl.ds(pl.multiple_of(c * half, half), half)
    sib_rows = pl.ds(pl.multiple_of((1 - c) * half, half), half)
    base_copies = [
        copy(mesh_base.at[sib_rows, :], base_s.at[i], b_send.at[0], b_recv.at[0], (g, d, sib)),
        copy(mesh_base.at[my_rows, :], base_s.at[i], b_send.at[1], b_recv.at[1], (g, d, xp)),
        copy(mesh_base.at[sib_rows, :], base_s.at[i], b_send.at[2], b_recv.at[2], (g, d, xs)),
    ]

    pl.semaphore_wait(barrier, len(peers))

    def launch(ks):
        for k in ks:
            to_x(k).start()
            to_sib(k).start()

    def relay(ks):
        for k in ks:
            to_x(k).wait_recv()
            fwd(k).start()

    def ready(ks):
        for k in ks:
            to_sib(k).wait_recv()
            fwd(k).wait_recv()

    launch([EMB, 0, 1])
    for b in base_copies:
        b.start()
    for k in range(n_w):
        wq[k, i] = sources[k][...]
    base_s[i] = mesh_base[my_rows, :]

    def build(src_ref, dst_ref, wt_ref, target_of, source_of, rows, cols, size, t):
        e = pl.ds(pl.multiple_of(t * size, size), size)
        tgt = target_of(lax.broadcasted_iota(jnp.int32, (rows, size), 0))
        dt = jnp.where(tgt == dst_ref[:, e], 1.0, 0.0).astype(BF)
        src = source_of(lax.broadcasted_iota(jnp.int32, (cols, size), 0))
        st = jnp.where(src == src_ref[:, e], wt_ref[:, e], 0.0).astype(BF)
        return mm_nt(dt, st)

    def mesh_order(m):
        return jnp.where(m < half, m + c * half, jnp.where(m < md, m - c * half, m))

    def enc_target(m):
        return jnp.where(m < half, m + c * half, m + (md - half))

    enc_size = min(CHUNK, enc_src.shape[1])
    enc_steps = enc_src.shape[1] // enc_size

    def build_enc(t):
        return build(
            enc_src, enc_slot, enc_wt, enc_target, lambda m: m, half + 4 * cap, gd, enc_size, t
        )

    if enc_steps == 1:
        a_enc[...] = build_enc(0).astype(BF)
    else:
        acc_enc[...] = build_enc(0)
        for t in range(1, enc_steps):
            acc_enc[...] += build_enc(t)
        a_enc[...] = acc_enc[...].astype(BF)
    launch([2, 3])

    def weight(k):
        return jnp.concatenate([wq[k, q] for q in range(4)], axis=1)

    def tiles(n, body):
        def step(t, _):
            body(pl.ds(pl.multiple_of(t * TILE, TILE), TILE))
            return 0

        lax.fori_loop(0, n // TILE, step, 0)

    relay([EMB, 0])
    ready([EMB])

    def embed(r):
        w = jnp.concatenate([emb_s[q] for q in range(4)], axis=1)[0:cin]
        grid_lat[r, :] = silu(mm_tn(grid_feat[:, r], w)).astype(BF)

    tiles(gd, embed)
    ready([0])

    def edge(r):
        sent[r, :] = silu(mm(grid_lat[r, :], weight(0))).astype(BF)

    tiles(gd, edge)

    slots = pl.ds(half, 4 * cap)
    def exchange(value, out_ref, in_ref, rows, send, recv):
        out_ref[...] = value.astype(BF)
        copies = []
        for j in range(4):
            peer = (g, lax.rem(d + offsets[j], n_dom), i)
            part = pl.ds(j * rows, rows)
            copies.append(copy(out_ref.at[part, :], in_ref.at[part, :], send.at[j], recv.at[j], peer))
            copies[-1].start()
        return copies

    enc_copies = exchange(mm(a_enc[slots, :], sent[...]), enc_out, enc_in, cap, e_send, e_recv)
    halo_copies = []

    def enc_local(r):
        esum[r, :] = mm(a_enc[r, :], sent[...])

    tiles(half, enc_local)
    relay([1])

    launch([4, 5])

    def pick(rows_ref, ref):
        n = ref.shape[0]
        row = rows_ref[pl.ds(d, 1), :].astype(F32)
        col = jnp.broadcast_to(row, (128, n)).T
        lane = lax.broadcasted_iota(jnp.int32, (n, 128), 1).astype(F32)
        for b in range(md // 128):
            shift = c * half if b * 128 < half else -c * half
            here = lane + (128 * b + shift).astype(F32)
            ref[:, b * 128 : (b + 1) * 128] = jnp.where(col == here, 1.0, 0.0).astype(BF)

    pick(halo_rows, pick_h)
    pick(dec_rows, pick_d)

    mesh_size = CHUNK
    mesh_chunks = mesh_src.shape[1] // mesh_size
    dec_size = dec_src.shape[1] // 2
    mesh_cols = acc_mesh.shape[1]

    def mesh_target(m):
        return m + c * half

    def dec_target(m):
        return m + i * quarter

    def build_mesh(t):
        return build(
            mesh_src, mesh_dst, mesh_wt, mesh_target, mesh_order, half, mesh_cols, mesh_size, t
        )

    def build_dec(t):
        return build(
            dec_src, dec_dst, dec_wt, dec_target, mesh_order, quarter, acc_dec.shape[1], dec_size, t
        )

    def mesh_step(t, _):
        acc_mesh[...] += build_mesh(t)
        return 0

    acc_mesh[...] = build_mesh(0)
    relay([2, 3])
    launch([6, 7, OUT])
    lax.fori_loop(1, mesh_chunks - 1, mesh_step, 0)
    relay([4, 5])

    for cp in enc_copies:
        cp.wait_recv()
    ready([1])
    for b in base_copies:
        b.wait_recv()

    def agg(r):
        m = lax.broadcasted_iota(jnp.int32, (TILE, 4 * cap), 0) + (c * half + r.start)
        place = jnp.where(m == enc_row[...], 1.0, 0.0).astype(BF)
        total = (esum[r, :] + mm(place, enc_in[...])).astype(BF)
        base = jnp.concatenate([base_s[q, r, :] for q in range(4)], axis=1).astype(F32)
        lat[r, :] = (base + silu(mm(total, weight(1)))).astype(BF)

    tiles(half, agg)

    share_copies = []

    def share(k, t):
        def body(r):
            msg[t, r, :] = silu(mm(lat[r, :], weight(k))).astype(BF)

        tiles(half, body)
        cp = copy(
            msg.at[t, pl.ds(0, half), :], msg.at[t, pl.ds(half, half), :],
            g_send.at[t], g_recv.at[t], (g, d, sib),
        )
        cp.start()
        share_copies.append(cp)
        return cp

    near, far = pl.ds(0, half), pl.ds(half, half)
    for l in range(layers):
        kw = 2 + 2 * l
        ready([kw])
        cp = share(kw, l)
        picked = mm(pick_h[:, 0:half], msg[l, near, :])
        if l == 0:
            a_mesh[...] = (acc_mesh[...] + build_mesh(mesh_chunks - 1)).astype(BF)
        else:
            acc_dec[...] += build_dec(1)
            a_dec[...] = acc_dec[...].astype(BF)

        def local(r, l=l):
            esum[r, :] = mm(a_mesh[r, 0:half], msg[l, near, :])

        tiles(half, local)
        cp.wait_recv()
        arriving = exchange(
            picked + mm(pick_h[:, half:md], msg[l, far, :]),
            halo_out.at[l], halo_in.at[l], hb, h_send.at[l], h_recv.at[l],
        )
        halo_copies += arriving

        def local(r, l=l):
            esum[r, :] += mm(a_mesh[r, half:md], msg[l, far, :])

        tiles(half, local)
        if l == 0:
            acc_dec[...] = build_dec(0)
            relay([6, 7, OUT])
        ready([kw + 1])
        for cp in arriving:
            cp.wait_recv()

        def update(r, l=l, kw=kw):
            total = (esum[r, :] + mm(a_mesh[r, md : md + 4 * hb], halo_in[l])).astype(BF)
            lat[r, :] = (lat[r, :].astype(F32) + silu(mm(total, weight(kw + 1)))).astype(BF)

        tiles(half, update)

    kd = n_w - 2
    ready([kd])
    cp = share(kd, layers)
    picked = mm(pick_d[:, 0:half], msg[layers, near, :])
    part = mm(a_dec[:, 0:half], msg[layers, near, :])
    ready([n_w - 1, OUT])
    cp.wait_recv()
    dec_copies = exchange(
        picked + mm(pick_d[:, half:md], msg[layers, far, :]), dec_out, dec_in, db, d_send, d_recv
    )
    part = part + mm(a_dec[:, half:md], msg[layers, far, :])
    for cp in dec_copies:
        cp.wait_recv()
    total = (part + mm(a_dec[:, md : md + 4 * db], dec_in[...])).astype(BF)
    mine = grid_lat[pl.ds(pl.multiple_of(i * quarter, quarter), quarter), :].astype(F32)
    new = (mine + silu(mm(total, weight(n_w - 1)))).astype(BF)
    head = jnp.concatenate([wo[q] for q in range(4)], axis=1)
    out[...] = mm_nt(head, new)[0:cin, :]

    for k in range(n_w + 2):
        to_sib(k).wait_send()
        to_x(k).wait_send()
        fwd(k).wait_send()
    for cp in base_copies + enc_copies + halo_copies + dec_copies + share_copies:
        cp.wait_send()


def per_device(n_dom, *args):
    args = (args[0].T,) + args[1:9] + (args[9].T,) + args[10:]
    grid_feat, mesh_base, w_msg = args[0], args[1], args[5]
    enc_row, halo_rows, dec_rows = args[13], args[17], args[21]
    cin, gd = grid_feat.shape
    md = mesh_base.shape[0]
    layers, width = w_msg.shape[0], w_msg.shape[1]
    half, quarter = md // 2, gd // 4
    n_enc, n_halo, n_dec = enc_row.shape[1], halo_rows.shape[1], dec_rows.shape[1]
    n_w = 4 + 2 * layers
    cin_pad = -(-cin // 128) * 128
    mesh_cols = md + -(-n_halo // 128) * 128
    dec_cols = md + -(-n_dec // 128) * 128
    V = pltpu.VMEM
    dma = pltpu.SemaphoreType.DMA
    scratch = [
        V((4, cin_pad, 128), BF),
        V((n_w, 4, width, 128), BF),
        V((4, cin_pad, 128), BF),
        V((4, half, 128), BF),
        V((gd, width), BF),
        V((gd, width), BF),
        V((half + n_enc, gd), BF),
        V((half + n_enc, gd), F32),
        V((half, mesh_cols), BF),
        V((half, mesh_cols), F32),
        V((quarter, dec_cols), BF),
        V((quarter, dec_cols), F32),
        V((n_halo, md), BF),
        V((n_dec, md), BF),
        V((n_enc, width), BF),
        V((n_enc, width), BF),
        V((half, width), F32),
        V((half, width), BF),
        V((layers + 1, md, width), BF),
        V((layers, n_halo, width), BF),
        V((layers, n_halo, width), BF),
        V((n_dec, width), BF),
        V((n_dec, width), BF),
        dma((n_w + 2,)), dma((n_w + 2,)), dma((n_w + 2,)), dma((n_w + 2,)), dma((n_w + 2,)), dma((n_w + 2,)),
        dma((3,)), dma((3,)),
        dma((4,)), dma((4,)), dma((layers, 4)), dma((layers, 4)), dma((4,)), dma((4,)),
        dma((layers + 1,)), dma((layers + 1,)),
    ]
    return pl.pallas_call(
        functools.partial(kernel, n_dom),
        out_shape=jax.ShapeDtypeStruct((cin, quarter), F32),
        in_specs=[pl.BlockSpec(memory_space=V)] * len(args),
        out_specs=pl.BlockSpec(memory_space=V),
        scratch_shapes=scratch,
        compiler_params=pltpu.CompilerParams(
            collective_id=0, has_side_effects=True, vmem_limit_bytes=56 * 1024 * 1024
        ),
    )(*args).T


def solution(mesh):
    in_specs = (
        P(("groups", "dom"), None),
        P(("groups", "dom"), "mp"),
        P(None, "mp"),
        P(None, "mp"),
        P(None, "mp"),
        P(None, None, "mp"),
        P(None, None, "mp"),
        P(None, "mp"),
        P(None, "mp"),
        P("mp", None),
        P("dom", None),
        P("dom", None),
        P("dom", None),
        P("dom", None),
        P("dom", None),
        P("dom", None),
        P("dom", None),
        P(),
        P("dom", None),
        P("dom", None),
        P("dom", None),
        P(),
    )
    out_specs = P(("groups", "dom", "mp"), None)
    return jax.shard_map(
        functools.partial(per_device, mesh.shape["dom"]),
        mesh=mesh,
        in_specs=in_specs,
        out_specs=out_specs,
        check_vma=False,
    )
```
